512 devices in a mesh: vv: 64 (over z, x, core), oo: 8 (over y).
Axes of the slice: x: 4, y: 8, z: 8, core: 2. Of those that a mesh axis runs over, the one named last changes fastest.
Arguments:
- amplitudes: bfloat16 [384, 32768], P(None, ('oo', 'vv')), may hold values from -6 to 6
- integrals: bfloat16 [32768, 32768], P('vv', 'oo'), may hold values from -0.078125 to 0.078125
- allowed: int32 [256, 256], P('vv', 'oo'), may hold values from 0 to 1, as said below
Outputs:
- ladder: bfloat16 [384, 32768], P('oo', 'vv')
The draws below stay inside these ranges and needn't reach their ends.
Inputs may be any that keep to these rules, and one draw needn't show every extreme that they name: `allowed`: each entry is 0 or 1; nothing about the number of ones may be relied on.
All inputs are finite; a program needn't handle non-finite values.
Results may differ from the reference program's by a relative error of at most 0.0015.
Values may be sent and summed in bfloat16 or wider, within the bound.
No kernel may reach another device: no remote copies, remote signals or barrier semaphores. Data moves between devices by JAX's collectives and lax.ppermute only.
A program may use at most 64 MiB of HBM per device.

```python
import jax
import jax.numpy as jnp
from jax import lax

OP = 384
BLK = 128
AB_DEV = 512
NPAIR = 32768
NBLK = 256
N_VV = 64


def draw_allowed(key, part):
    key = jax.random.fold_in(key, 7)
    first, second = jax.random.split(key)
    labels = jax.random.randint(first, (NBLK,), 0, 8)
    same = (labels[:, None] == labels[None, :]).astype(jnp.int32)
    flips = (jax.random.randint(second, (NBLK, NBLK), 0, 16) == 0).astype(jnp.int32)
    return (same + flips - 2 * same * flips).astype(jnp.int32)


def steps_of(own_key, extent, pieces, smallest, high):
    factor_of, own = 1.0, jax.random.fold_in(own_key, 6)
    for dim, shards_of in pieces:
        draws = jnp.exp(jax.random.uniform(jax.random.fold_in(own, dim), (shards_of,), jnp.float32, smallest / len(pieces), high / len(pieces)))
        factor_of = factor_of * jnp.repeat(draws, extent[dim] // shards_of).reshape([-1 if axis == dim else 1 for axis in range(len(extent))])
    return factor_of


def scatter_about(stream_key, shape, spread, bound, cuts=(), kind=jnp.bfloat16):
    gain = steps_of(stream_key, shape, cuts, -0.22, 0.18) if cuts else 1.0
    array = jax.random.normal(stream_key, shape, jnp.float32) * spread * gain
    return jnp.minimum(jnp.maximum(array, -bound), bound).astype(kind)


def setup_inputs(seed: int = 0) -> dict:
    streams_of = jax.random.split(jax.random.key(seed), 4)
    return {
        "amplitudes": scatter_about(streams_of[0], (OP, NPAIR), 1.0, 6.0, ((1, 512),)),
        "integrals": scatter_about(streams_of[1], (NPAIR, NPAIR), (NPAIR // 6) ** -0.5, 0.078125, ((0, 64), (1, 8))),
        "allowed": draw_allowed(jax.random.fold_in(streams_of[3], 71), 0),
    }


def reference(amplitudes, integrals, allowed):
    per_row = AB_DEV // BLK

    def one(index):
        rows = lax.dynamic_slice_in_dim(integrals, index * AB_DEV, AB_DEV, 0)
        flags = lax.dynamic_slice_in_dim(allowed, index * per_row, per_row, 0)
        tiles = jnp.repeat(jnp.repeat(flags, BLK, axis=0), BLK, axis=1).astype(jnp.bfloat16)
        masked = rows * tiles
        return lax.dot_general(amplitudes, masked, (((1,), (1,)), ((), ())), preferred_element_type=jnp.float32)

    blocks = lax.map(one, jnp.arange(N_VV, dtype=jnp.int32))
    whole = jnp.transpose(blocks, (1, 0, 2)).reshape(OP, NPAIR)
    return whole.astype(jnp.bfloat16)
```

```python
import jax
import jax.numpy as jnp
from jax import lax
from jax.experimental import pallas as pl
from jax.experimental.pallas import tpu as pltpu
from jax.sharding import Mesh, PartitionSpec as P

OP = 384
BLK = 128
NZ, NX, NC, NY = 8, 4, 2, 8
ROWS = 512
COLS = 4096
HALF = OP // 2
SEG = OP // (NY * NC)
SCALE = 32.0


def pick(which, part):
    shape = (OP, 128)
    source = lax.broadcasted_iota(jnp.int32, shape, 0)
    lane = lax.broadcasted_iota(jnp.int32, shape, 1)
    if part == 0:
        wanted = lane
    elif part == 1:
        wanted = jnp.where(lane < 64, lane + 128, -1)
    else:
        wanted = jnp.where(lane >= 64, lane + 64, -1)
    y = sum((wanted >= SEG * k).astype(jnp.int32) for k in range(1, NY))
    row = wanted + y * SEG + which * SEG
    hit = (source == row) & (wanted >= 0)
    return jnp.where(hit, 1.0, 0.0).astype(jnp.bfloat16)


def pack_kernel(a_ref, out_ref):
    a = a_ref[...]
    f32 = jnp.float32
    for core in range(NC):
        head = jnp.dot(a, pick(core, 0), preferred_element_type=f32)
        tail = jnp.dot(a[:32], pick(core, 1), preferred_element_type=f32)
        tail += jnp.dot(a[32:], pick(core, 2), preferred_element_type=f32)
        head, tail = head.astype(jnp.bfloat16), tail.astype(jnp.bfloat16)
        for z in range(NZ):
            out_ref[z, core, :64] = head
            out_ref[z, core, 64:] = tail


def pack(a):
    return pl.pallas_call(
        pack_kernel,
        out_shape=jax.ShapeDtypeStruct((NZ, NC, 96, 128), jnp.bfloat16),
        cost_estimate=pl.CostEstimate(flops=2 * 64 * OP * 512, bytes_accessed=450_000, transcendentals=0),
    )(a)


def mask_kernel(allowed_ref, m_ref, out_ref):
    row = pl.program_id(0)
    for j in range(COLS // BLK):
        keep = allowed_ref[row, j] != 0
        cols = slice(j * BLK, (j + 1) * BLK)
        tile = m_ref[:, cols]
        out_ref[:, cols] = jnp.where(keep, tile, jnp.zeros_like(tile))


def mask(allowed, m):
    return pl.pallas_call(
        mask_kernel,
        grid=(ROWS // BLK,),
        in_specs=[
            pl.BlockSpec(memory_space=pltpu.SMEM),
            pl.BlockSpec((BLK, COLS), lambda i: (i, 0)),
        ],
        out_specs=pl.BlockSpec((BLK, COLS), lambda i: (i, 0)),
        out_shape=jax.ShapeDtypeStruct((ROWS, COLS), jnp.bfloat16),
        cost_estimate=pl.CostEstimate(flops=ROWS * COLS, bytes_accessed=4 * ROWS * COLS, transcendentals=0),
    )(allowed, m)


KC = 4
KW = COLS // KC
ZC = NZ // KC


def dot_kernel(g_ref, own_ref, other_ref, out_ref, w_ref, acc_ref):
    step = pl.program_id(0)
    for z in range(ZC):
        for x in range(NX):
            for c in range(NC):
                at = z * 512 + x * 128 + c * 64
                w_ref[at : at + 64, :128] = g_ref[x, z * NC + c, :64]
                tail = g_ref[x, z * NC + c, 64:]
                w_ref[at : at + 32, 128:] = tail
                w_ref[at + 32 : at + 64, 128:] = jnp.concatenate([tail[:, 64:], tail[:, :64]], axis=1)
    w = w_ref[...]

    @pl.when(step == 0)
    def _():
        acc_ref[...] = jnp.zeros_like(acc_ref)

    for i, m_ref in enumerate((own_ref, other_ref)):
        acc_ref[i] += jnp.dot(m_ref[...], w, preferred_element_type=jnp.float32)

    @pl.when(step == KC - 1)
    def _():
        own, other = [(acc_ref[i] * SCALE).T[:HALF] for i in range(NC)]
        leads = lax.axis_index("c") == 0
        sums = jnp.where(leads, own, other), jnp.where(leads, other, own)
        for y in range(NY):
            for c in range(NC):
                at = (y * NC + c) * SEG
                out_ref[at : at + SEG] = sums[c][y * SEG : (y + 1) * SEG]


def dots(g, own, other):
    return pl.pallas_call(
        dot_kernel,
        grid=(KC,),
        in_specs=[
            pl.BlockSpec((NX, ZC * NC, 96, 128), lambda k: (0, k, 0, 0)),
            pl.BlockSpec((ROWS, KW), lambda k: (0, k)),
            pl.BlockSpec((ROWS, KW), lambda k: (0, k)),
        ],
        out_specs=pl.BlockSpec((OP, ROWS), lambda k: (0, 0)),
        out_shape=jax.ShapeDtypeStruct((OP, ROWS), jnp.float32),
        scratch_shapes=[
            pltpu.VMEM((KW, 256), jnp.bfloat16),
            pltpu.VMEM((NC, ROWS, 256), jnp.float32),
        ],
        compiler_params=pltpu.CompilerParams(vmem_limit_bytes=24 << 20),
        cost_estimate=pl.CostEstimate(flops=2 * OP * ROWS * COLS, bytes_accessed=10 << 20, transcendentals=0),
    )(g, own, other)


def shards(amplitudes, integrals, allowed):
    pieces = pack(amplitudes.T)
    over_z = lax.all_to_all(pieces.reshape(NZ * NC * 96, 128), ("z", "c"), 0, 0, tiled=True)
    own = mask(allowed, integrals)
    other = lax.ppermute(own, "c", [(0, 1), (1, 0)])
    copies = jnp.broadcast_to(over_z[None], (NX, NZ * NC * 96, 128)).reshape(-1, 128)
    over_x = lax.all_to_all(copies, "x", 0, 0, tiled=True)
    g = over_x.reshape(NX, NZ * NC, 96, 128)
    partial_sums = dots(g, own, other).astype(jnp.float16)
    landed = lax.all_to_all(partial_sums, ("y", "c"), 0, 0, tiled=True)
    total = jnp.sum(landed.reshape(NY, 2 * SEG, ROWS).astype(jnp.float32), axis=0)
    return (total * (1.0 / SCALE)).astype(jnp.bfloat16)


def solution(mesh):
    fine = Mesh(mesh.devices.reshape(NZ, NX, NC, NY), ("z", "x", "c", "y"))
    vv = ("z", "x", "c")
    placed = (P(None, ("y",) + vv), P(vv, "y"), P(vv, "y"))
    return jax.shard_map(shards, mesh=fine, in_specs=placed, out_specs=P("y", vv), check_vma=False)
```

```python
import jax
import jax.numpy as jnp
from jax import lax
from jax.experimental import pallas as pl
from jax.experimental.pallas import tpu as pltpu
from jax.sharding import Mesh, PartitionSpec as P

OP = 384
BLK = 128
NZ, NX, NC, NY = 8, 4, 2, 8
ROWS = 512
COLS = 4096
HALF = OP // 2
SEG = OP // (NY * NC)
SCALE = 32.0


def pick(which, part):
    lane = lax.broadcasted_iota(jnp.int32, (1, 128), 1)
    if part == 0:
        wanted, used = lane, lane >= 0
    elif part == 1:
        wanted, used = lane + 128, lane < 64
    else:
        wanted, used = lane + 64, lane >= 64
    y = sum((wanted >= SEG * k).astype(jnp.int32) for k in range(1, NY))
    row = jnp.where(used, wanted + (y + which) * SEG, -1)
    source = lax.broadcasted_iota(jnp.int32, (OP, 128), 0)
    return jnp.where(source == row, 1.0, 0.0).astype(jnp.bfloat16)


def pack_kernel(a_ref, out_ref):
    a = a_ref[...]
    f32 = jnp.float32
    for core in range(NC):
        head = jnp.dot(a, pick(core, 0), preferred_element_type=f32)
        tail = jnp.dot(a[:32], pick(core, 1), preferred_element_type=f32)
        tail += jnp.dot(a[32:], pick(core, 2), preferred_element_type=f32)
        head, tail = head.astype(jnp.bfloat16), tail.astype(jnp.bfloat16)
        for z in range(NZ):
            out_ref[z, core, :64] = head
            out_ref[z, core, 64:] = tail


def pack(a):
    return pl.pallas_call(
        pack_kernel,
        out_shape=jax.ShapeDtypeStruct((NZ, NC, 96, 128), jnp.bfloat16),
        cost_estimate=pl.CostEstimate(flops=2 * 64 * OP * 512, bytes_accessed=450_000, transcendentals=0),
    )(a)


def mask_kernel(allowed_ref, m_ref, out_ref):
    @pl.loop(0, ROWS // BLK)
    def _(i):
        rows = pl.ds(pl.multiple_of(i * BLK, BLK), BLK)
        for j in range(COLS // BLK):
            keep = allowed_ref[i, j] != 0
            cols = slice(j * BLK, (j + 1) * BLK)
            tile = m_ref[rows, cols]
            out_ref[rows, cols] = jnp.where(keep, tile, jnp.zeros_like(tile))


def mask(allowed, m):
    return pl.pallas_call(
        mask_kernel,
        in_specs=[pl.BlockSpec(memory_space=pltpu.SMEM), pl.BlockSpec(memory_space=pltpu.VMEM)],
        out_specs=pl.BlockSpec(memory_space=pltpu.VMEM),
        out_shape=jax.ShapeDtypeStruct((ROWS, COLS), jnp.bfloat16),
        compiler_params=pltpu.CompilerParams(vmem_limit_bytes=16 << 20),
        cost_estimate=pl.CostEstimate(flops=ROWS * COLS, bytes_accessed=4 * ROWS * COLS, transcendentals=0),
    )(allowed, m)


KW = 512


def dot_kernel(g_ref, own_ref, other_ref, out_ref, w_ref, acc_ref):
    for z in range(NZ):
        for x in range(NX):
            for c in range(NC):
                at = x * 128 + c * 64
                w_ref[at : at + 64, :128] = g_ref[x, z * NC + c, :64]
                tail = g_ref[x, z * NC + c, 64:]
                w_ref[at : at + 32, 128:] = tail
                w_ref[at + 32 : at + 64, 128:] = jnp.concatenate([tail[:, 64:], tail[:, :64]], axis=1)
        w = w_ref[...]
        for i, m_ref in enumerate((own_ref, other_ref)):
            part = jnp.dot(m_ref[:, z * KW : (z + 1) * KW], w, preferred_element_type=jnp.float32)
            if z == 0:
                acc_ref[i] = part
            else:
                acc_ref[i] += part
    own, other = [(acc_ref[i] * SCALE).T[:HALF] for i in range(NC)]
    leads = lax.axis_index("c") == 0
    sums = jnp.where(leads, own, other), jnp.where(leads, other, own)
    for y in range(NY):
        for c in range(NC):
            at = (y * NC + c) * SEG
            out_ref[at : at + SEG] = sums[c][y * SEG : (y + 1) * SEG]


def dots(g, own, other):
    return pl.pallas_call(
        dot_kernel,
        in_specs=[pl.BlockSpec(memory_space=pltpu.VMEM)] * 3,
        out_specs=pl.BlockSpec(memory_space=pltpu.VMEM),
        out_shape=jax.ShapeDtypeStruct((OP, ROWS), jnp.float32),
        scratch_shapes=[
            pltpu.VMEM((KW, 256), jnp.bfloat16),
            pltpu.VMEM((NC, ROWS, 256), jnp.float32),
        ],
        compiler_params=pltpu.CompilerParams(vmem_limit_bytes=24 << 20),
        cost_estimate=pl.CostEstimate(flops=2 * OP * ROWS * COLS, bytes_accessed=10 << 20, transcendentals=0),
    )(g, own, other)


def shards(amplitudes, integrals, allowed):
    pieces = pack(amplitudes.T)
    over_z = lax.all_to_all(pieces.reshape(NZ * NC * 96, 128), ("z", "c"), 0, 0, tiled=True)
    over_z, allowed = lax.optimization_barrier((over_z, allowed))
    own = mask(allowed, integrals)
    other = lax.ppermute(own, "c", [(0, 1), (1, 0)])
    copies = jnp.broadcast_to(over_z[None], (NX, NZ * NC * 96, 128)).reshape(-1, 128)
    over_x = lax.all_to_all(copies, "x", 0, 0, tiled=True)
    g = over_x.reshape(NX, NZ * NC, 96, 128)
    partial_sums = dots(g, own, other).astype(jnp.float16)
    landed = lax.all_to_all(partial_sums, ("y", "c"), 0, 0, tiled=True)
    total = jnp.sum(landed.reshape(NY, 2 * SEG, ROWS).astype(jnp.float32), axis=0)
    return (total * (1.0 / SCALE)).astype(jnp.bfloat16)


def solution(mesh):
    fine = Mesh(mesh.devices.reshape(NZ, NX, NC, NY), ("z", "x", "c", "y"))
    vv = ("z", "x", "c")
    placed = (P(None, ("y",) + vv), P(vv, "y"), P(vv, "y"))
    return jax.shard_map(shards, mesh=fine, in_specs=placed, out_specs=P("y", vv), check_vma=False)
```

```python
import jax
import jax.numpy as jnp
from jax import lax
from jax.experimental import pallas as pl
from jax.experimental.pallas import tpu as pltpu
from jax.sharding import Mesh, PartitionSpec as P

OP = 384
BLK = 128
NZ, NX, NC, NY = 8, 4, 2, 8
ROWS = 512
COLS = 4096
HALF = OP // 2
SEG = OP // (NY * NC)
SCALE = 32.0


def pick(which, part):
    lane = lax.broadcasted_iota(jnp.int32, (1, 128), 1)
    if part == 0:
        wanted, used = lane, lane >= 0
    elif part == 1:
        wanted, used = lane + 128, lane < 64
    else:
        wanted, used = lane + 64, lane >= 64
    y = sum((wanted >= SEG * k).astype(jnp.int32) for k in range(1, NY))
    row = jnp.where(used, wanted + (y + which) * SEG, -1)
    source = lax.broadcasted_iota(jnp.int32, (OP, 128), 0)
    return jnp.where(source == row, 1.0, 0.0).astype(jnp.bfloat16)


def pack_kernel(a_ref, out_ref):
    a = a_ref[...]
    f32 = jnp.float32
    for core in range(NC):
        head = jnp.dot(a, pick(core, 0), preferred_element_type=f32)
        tail = jnp.dot(a[:32], pick(core, 1), preferred_element_type=f32)
        tail += jnp.dot(a[32:], pick(core, 2), preferred_element_type=f32)
        head, tail = head.astype(jnp.bfloat16), tail.astype(jnp.bfloat16)
        for z in range(NZ):
            out_ref[z, core, :64] = head
            out_ref[z, core, 64:] = tail


def pack(a):
    return pl.pallas_call(
        pack_kernel,
        out_shape=jax.ShapeDtypeStruct((NZ, NC, 96, 128), jnp.bfloat16),
        cost_estimate=pl.CostEstimate(flops=2 * 64 * OP * 512, bytes_accessed=450_000, transcendentals=0),
    )(a)


def mask_kernel(allowed_ref, m_ref, out_ref):
    @pl.loop(0, ROWS // BLK)
    def _(i):
        rows = pl.ds(pl.multiple_of(i * BLK, BLK), BLK)
        for j in range(COLS // BLK):
            keep = allowed_ref[i, j] != 0
            cols = slice(j * BLK, (j + 1) * BLK)
            tile = m_ref[rows, cols]
            out_ref[rows, cols] = jnp.where(keep, tile, jnp.zeros_like(tile))


def mask(allowed, m):
    return pl.pallas_call(
        mask_kernel,
        in_specs=[pl.BlockSpec(memory_space=pltpu.SMEM), pl.BlockSpec(memory_space=pltpu.VMEM)],
        out_specs=pl.BlockSpec(memory_space=pltpu.VMEM),
        out_shape=jax.ShapeDtypeStruct((ROWS, COLS), jnp.bfloat16),
        compiler_params=pltpu.CompilerParams(vmem_limit_bytes=16 << 20),
        cost_estimate=pl.CostEstimate(flops=ROWS * COLS, bytes_accessed=4 * ROWS * COLS, transcendentals=0),
    )(allowed, m)


def spread(block_ref, w_ref):
    for zc in range(NZ * NC):
        at = zc * 64
        w_ref[at : at + 64, :128] = block_ref[zc, :64]
        tail = block_ref[zc, 64:]
        w_ref[at : at + 32, 128:] = tail
        w_ref[at + 32 : at + 64, 128:] = jnp.concatenate([tail[:, 64:], tail[:, :64]], axis=1)


def block_dot(m_ref, w, x):
    at = [pl.ds(pl.multiple_of(z * NX * BLK + x * BLK, BLK), BLK) for z in range(NZ)]
    m = jnp.concatenate([m_ref[:, cols] for cols in at], axis=1)
    return jnp.dot(m, w, preferred_element_type=jnp.float32)


def source(shift):
    return lax.rem(lax.axis_index("x") + (NX - shift), NX)


def first_kernel(shifts, *refs):
    block_refs = refs[: len(shifts)]
    own_ref, other_ref, acc_ref, w_ref = refs[len(shifts) :]
    for n, shift in enumerate(shifts):
        spread(block_refs[n], w_ref)
        w = w_ref[...]
        for i, m_ref in enumerate((own_ref, other_ref)):
            part = block_dot(m_ref, w, source(shift))
            acc_ref[i] = part if n == 0 else acc_ref[i] + part


def last_kernel(shift, block_ref, in_ref, own_ref, other_ref, out_ref, w_ref, acc_ref):
    spread(block_ref, w_ref)
    w = w_ref[...]
    for i, m_ref in enumerate((own_ref, other_ref)):
        acc_ref[i] = in_ref[i] + block_dot(m_ref, w, source(shift))
    own, other = [(acc_ref[i] * SCALE).T[:HALF] for i in range(NC)]
    leads = lax.axis_index("c") == 0
    sums = jnp.where(leads, own, other), jnp.where(leads, other, own)
    for y in range(NY):
        for c in range(NC):
            at = (y * NC + c) * SEG
            out_ref[at : at + SEG] = sums[c][y * SEG : (y + 1) * SEG]


ACC = (NC, ROWS, 256)
WIDE = NZ * NC * 64


def first_dots(shifts, blocks, own, other):
    def first(*refs):
        first_kernel(shifts, *refs)

    return pl.pallas_call(
        first,
        in_specs=[pl.BlockSpec(memory_space=pltpu.VMEM)] * (len(shifts) + 2),
        out_specs=pl.BlockSpec(memory_space=pltpu.VMEM),
        out_shape=jax.ShapeDtypeStruct(ACC, jnp.float32),
        scratch_shapes=[pltpu.VMEM((WIDE, 256), jnp.bfloat16)],
        compiler_params=pltpu.CompilerParams(vmem_limit_bytes=16 << 20),
        cost_estimate=pl.CostEstimate(flops=OP * ROWS * COLS, bytes_accessed=3 << 20, transcendentals=0),
    )(*blocks, own, other)


def last_dots(shift, block, acc, own, other):
    def last(*refs):
        last_kernel(shift, *refs)

    return pl.pallas_call(
        last,
        in_specs=[pl.BlockSpec(memory_space=pltpu.VMEM)] * 4,
        out_specs=pl.BlockSpec(memory_space=pltpu.VMEM),
        out_shape=jax.ShapeDtypeStruct((OP, ROWS), jnp.float32),
        scratch_shapes=[pltpu.VMEM((WIDE, 256), jnp.bfloat16), pltpu.VMEM(ACC, jnp.float32)],
        compiler_params=pltpu.CompilerParams(vmem_limit_bytes=16 << 20),
        cost_estimate=pl.CostEstimate(flops=OP * ROWS * COLS // 2, bytes_accessed=3 << 20, transcendentals=0),
    )(block, acc, own, other)


SHIFTS = (2, 1, 3)


def shards(amplitudes, integrals, allowed):
    swap = [(0, 1), (1, 0)]
    raw = lax.ppermute(integrals, "c", swap)
    pieces = pack(amplitudes.T)
    over_z = lax.all_to_all(pieces.reshape(NZ * NC * 96, 128), ("z", "c"), 0, 0, tiled=True)
    block = over_z.reshape(NZ * NC, 96, 128)
    far, right, left = [lax.ppermute(block, "x", [(i, (i + d) % NX) for i in range(NX)]) for d in SHIFTS]
    block, allowed = lax.optimization_barrier((block, allowed))
    own = mask(allowed, integrals)
    other = mask(lax.ppermute(allowed, "c", swap), raw)
    acc = first_dots((0, 1, 3), (block, right, left), own, other)
    partial_sums = last_dots(2, far, acc, own, other).astype(jnp.float16)
    landed = lax.all_to_all(partial_sums, ("y", "c"), 0, 0, tiled=True)
    total = jnp.sum(landed.reshape(NY, 2 * SEG, ROWS).astype(jnp.float32), axis=0)
    return (total * (1.0 / SCALE)).astype(jnp.bfloat16)


def solution(mesh):
    fine = Mesh(mesh.devices.reshape(NZ, NX, NC, NY), ("z", "x", "c", "y"))
    vv = ("z", "x", "c")
    placed = (P(None, ("y",) + vv), P(vv, "y"), P(vv, "y"))
    return jax.shard_map(shards, mesh=fine, in_specs=placed, out_specs=P("y", vv), check_vma=False)
```

```python
import jax
import jax.numpy as jnp
from jax import lax
from jax.experimental import pallas as pl
from jax.experimental.pallas import tpu as pltpu
from jax.sharding import Mesh, PartitionSpec as P

OP = 384
BLK = 128
NZ, NX, NC, NY = 8, 4, 2, 8
ROWS = 512
COLS = 4096
HALF = OP // 2
SEG = OP // (NY * NC)
SCALE = 32.0


def pick():
    lane = lax.broadcasted_iota(jnp.int32, (1, 512), 1)
    head = lane < 256
    core = jnp.where(head, lane // 128, (lane - 256) // 128)
    place = jnp.where(head, lane % 128, 128 + lane % 64)
    row = (place // SEG) * (NC * SEG) + core * SEG + place % SEG
    source = lax.broadcasted_iota(jnp.int32, (OP, 512), 0)
    return jnp.where(source == row, 1.0, 0.0).astype(jnp.bfloat16)


def pack_kernel(a_ref, out_ref):
    picked = jnp.dot(a_ref[...], pick(), preferred_element_type=jnp.float32)
    low = lax.broadcasted_iota(jnp.int32, (32, 128), 1) < 64
    for core in range(NC):
        head = picked[:, core * 128 : (core + 1) * 128].astype(jnp.bfloat16)
        both = picked[:, 256 + core * 128 : 256 + (core + 1) * 128]
        tail = jnp.where(low, both[:32], both[32:]).astype(jnp.bfloat16)
        for z in range(NZ):
            out_ref[z, core, :64] = head
            out_ref[z, core, 64:] = tail


def pack(a):
    return pl.pallas_call(
        pack_kernel,
        out_shape=jax.ShapeDtypeStruct((NZ, NC, 96, 128), jnp.bfloat16),
        in_specs=[pl.BlockSpec(memory_space=pltpu.VMEM)],
        out_specs=pl.BlockSpec(memory_space=pltpu.VMEM),
        compiler_params=pltpu.CompilerParams(vmem_limit_bytes=4 << 20),
        cost_estimate=pl.CostEstimate(flops=2 * 64 * OP * 512, bytes_accessed=450_000, transcendentals=0),
    )(a)


def mask_kernel(allowed_ref, m_ref, out_ref):
    @pl.loop(0, ROWS // BLK)
    def _(i):
        rows = pl.ds(pl.multiple_of(i * BLK, BLK), BLK)
        for j in range(COLS // BLK):
            keep = allowed_ref[i, j] != 0
            cols = slice(j * BLK, (j + 1) * BLK)
            tile = m_ref[rows, cols]
            out_ref[rows, cols] = jnp.where(keep, tile, jnp.zeros_like(tile))


def mask(allowed, m):
    return pl.pallas_call(
        mask_kernel,
        in_specs=[pl.BlockSpec(memory_space=pltpu.SMEM), pl.BlockSpec(memory_space=pltpu.VMEM)],
        out_specs=pl.BlockSpec(memory_space=pltpu.VMEM),
        out_shape=jax.ShapeDtypeStruct((ROWS, COLS), jnp.bfloat16),
        compiler_params=pltpu.CompilerParams(vmem_limit_bytes=16 << 20),
        cost_estimate=pl.CostEstimate(flops=ROWS * COLS, bytes_accessed=4 * ROWS * COLS, transcendentals=0),
    )(allowed, m)


def spread(block_ref, w_ref):
    for zc in range(NZ * NC):
        at = zc * 64
        w_ref[at : at + 64, :128] = block_ref[zc, :64]
        tail = block_ref[zc, 64:]
        w_ref[at : at + 32, 128:] = tail
        w_ref[at + 32 : at + 64, 128:] = jnp.concatenate([tail[:, 64:], tail[:, :64]], axis=1)


def block_dot(m_ref, w, x):
    at = [pl.ds(pl.multiple_of(z * NX * BLK + x * BLK, BLK), BLK) for z in range(NZ)]
    m = jnp.concatenate([m_ref[:, cols] for cols in at], axis=1)
    return jnp.dot(m, w, preferred_element_type=jnp.float32)


def source(shift):
    return lax.rem(lax.axis_index("x") + (NX - shift), NX)


def some_kernel(shifts, *refs):
    block_refs = refs[: len(shifts)]
    own_ref, other_ref, acc_ref, w_ref = refs[-4:]
    before_ref = refs[len(shifts)] if len(refs) > len(shifts) + 4 else None
    for n, shift in enumerate(shifts):
        spread(block_refs[n], w_ref)
        w = w_ref[...]
        for i, m_ref in enumerate((own_ref, other_ref)):
            part = block_dot(m_ref, w, source(shift))
            if n > 0:
                part += acc_ref[i]
            elif before_ref is not None:
                part += before_ref[i]
            acc_ref[i] = part


def last_kernel(shift, block_ref, in_ref, own_ref, other_ref, out_ref, w_ref, acc_ref):
    spread(block_ref, w_ref)
    w = w_ref[...]
    for i, m_ref in enumerate((own_ref, other_ref)):
        acc_ref[i] = in_ref[i] + block_dot(m_ref, w, source(shift))
    own, other = [(acc_ref[i] * SCALE).T[:HALF] for i in range(NC)]
    leads = lax.axis_index("c") == 0
    sums = jnp.where(leads, own, other), jnp.where(leads, other, own)
    for y in range(NY):
        for c in range(NC):
            at = (y * NC + c) * SEG
            out_ref[at : at + SEG] = sums[c][y * SEG : (y + 1) * SEG]


ACC = (NC, ROWS, 256)
WIDE = NZ * NC * 64


def some_dots(shifts, blocks, before, own, other):
    def some(*refs):
        some_kernel(shifts, *refs)

    return pl.pallas_call(
        some,
        in_specs=[pl.BlockSpec(memory_space=pltpu.VMEM)] * (len(shifts) + len(before) + 2),
        out_specs=pl.BlockSpec(memory_space=pltpu.VMEM),
        out_shape=jax.ShapeDtypeStruct(ACC, jnp.float32),
        scratch_shapes=[pltpu.VMEM((WIDE, 256), jnp.bfloat16)],
        compiler_params=pltpu.CompilerParams(vmem_limit_bytes=16 << 20),
        cost_estimate=pl.CostEstimate(
            flops=len(shifts) * OP * ROWS * COLS // 2, bytes_accessed=3 << 20, transcendentals=0
        ),
    )(*blocks, *before, own, other)


def last_dots(shift, block, acc, own, other):
    def last(*refs):
        last_kernel(shift, *refs)

    return pl.pallas_call(
        last,
        in_specs=[pl.BlockSpec(memory_space=pltpu.VMEM)] * 4,
        out_specs=pl.BlockSpec(memory_space=pltpu.VMEM),
        out_shape=jax.ShapeDtypeStruct((OP, ROWS), jnp.float32),
        scratch_shapes=[pltpu.VMEM((WIDE, 256), jnp.bfloat16), pltpu.VMEM(ACC, jnp.float32)],
        compiler_params=pltpu.CompilerParams(vmem_limit_bytes=16 << 20),
        cost_estimate=pl.CostEstimate(flops=OP * ROWS * COLS // 2, bytes_accessed=3 << 20, transcendentals=0),
    )(block, acc, own, other)


SHIFTS = (2, 1, 3)


def shards(amplitudes, integrals, allowed):
    swap = [(0, 1), (1, 0)]
    raw = lax.ppermute(integrals, "c", swap)
    pieces = pack(amplitudes.T)
    over_z = lax.all_to_all(pieces.reshape(NZ * NC * 96, 128), ("z", "c"), 0, 0, tiled=True)
    block = over_z.reshape(NZ * NC, 96, 128)
    far, right, left = [lax.ppermute(block, "x", [(i, (i + d) % NX) for i in range(NX)]) for d in SHIFTS]
    block, allowed = lax.optimization_barrier((block, allowed))
    own = mask(allowed, integrals)
    other = mask(lax.ppermute(allowed, "c", swap), raw)
    acc = some_dots((0,), (block,), (), own, other)
    acc = some_dots((2, 1), (far, right), (acc,), own, other)
    partial_sums = last_dots(3, left, acc, own, other).astype(jnp.float16)
    landed = lax.all_to_all(partial_sums, ("y", "c"), 0, 0, tiled=True)
    total = jnp.sum(landed.reshape(NY, 2 * SEG, ROWS).astype(jnp.float32), axis=0)
    return (total * (1.0 / SCALE)).astype(jnp.bfloat16)


def solution(mesh):
    fine = Mesh(mesh.devices.reshape(NZ, NX, NC, NY), ("z", "x", "c", "y"))
    vv = ("z", "x", "c")
    placed = (P(None, ("y",) + vv), P(vv, "y"), P(vv, "y"))
    return jax.shard_map(shards, mesh=fine, in_specs=placed, out_specs=P("y", vv), check_vma=False)
```

```python
import jax
import jax.numpy as jnp
from jax import lax
from jax.experimental import pallas as pl
from jax.experimental.pallas import tpu as pltpu
from jax.sharding import Mesh, PartitionSpec as P

OP = 384
BLK = 128
NZ, NX, NC, NY = 8, 4, 2, 8
ROWS = 512
COLS = 4096
HALF = OP // 2
SEG = OP // (NY * NC)
SCALE = 32.0


def pick():
    lane = lax.broadcasted_iota(jnp.int32, (1, 512), 1)
    head = lane < 256
    core = jnp.where(head, lane // 128, (lane - 256) // 128)
    place = jnp.where(head, lane % 128, 128 + lane % 64)
    row = (place // SEG) * (NC * SEG) + core * SEG + place % SEG
    source = lax.broadcasted_iota(jnp.int32, (OP, 512), 0)
    return jnp.where(source == row, 1.0, 0.0).astype(jnp.bfloat16)


def pack_kernel(a_ref, out_ref):
    picked = jnp.dot(a_ref[...], pick(), preferred_element_type=jnp.float32)
    low = lax.broadcasted_iota(jnp.int32, (32, 128), 1) < 64
    for core in range(NC):
        head = picked[:, core * 128 : (core + 1) * 128].astype(jnp.bfloat16)
        both = picked[:, 256 + core * 128 : 256 + (core + 1) * 128]
        tail = jnp.where(low, both[:32], both[32:]).astype(jnp.bfloat16)
        for z in range(NZ):
            out_ref[z, core, :64] = head
            out_ref[z, core, 64:] = tail


def pack(a):
    return pl.pallas_call(
        pack_kernel,
        out_shape=jax.ShapeDtypeStruct((NZ, NC, 96, 128), jnp.bfloat16),
        in_specs=[pl.BlockSpec(memory_space=pltpu.VMEM)],
        out_specs=pl.BlockSpec(memory_space=pltpu.VMEM),
        compiler_params=pltpu.CompilerParams(vmem_limit_bytes=4 << 20),
        cost_estimate=pl.CostEstimate(flops=2 * 64 * OP * 512, bytes_accessed=450_000, transcendentals=0),
    )(a)


def mask_kernel(allowed_ref, m_ref, out_ref):
    @pl.loop(0, ROWS // BLK)
    def _(i):
        rows = pl.ds(pl.multiple_of(i * BLK, BLK), BLK)
        for j in range(COLS // BLK):
            keep = allowed_ref[i, j] != 0
            cols = slice(j * BLK, (j + 1) * BLK)
            tile = m_ref[rows, cols]
            out_ref[rows, cols] = jnp.where(keep, tile, jnp.zeros_like(tile))


def mask(allowed, m):
    return pl.pallas_call(
        mask_kernel,
        in_specs=[pl.BlockSpec(memory_space=pltpu.SMEM), pl.BlockSpec(memory_space=pltpu.VMEM)],
        out_specs=pl.BlockSpec(memory_space=pltpu.VMEM),
        out_shape=jax.ShapeDtypeStruct((ROWS, COLS), jnp.bfloat16),
        compiler_params=pltpu.CompilerParams(vmem_limit_bytes=16 << 20),
        cost_estimate=pl.CostEstimate(flops=ROWS * COLS, bytes_accessed=4 * ROWS * COLS, transcendentals=0),
    )(allowed, m)


def spread(block_ref, w_ref):
    for zc in range(NZ * NC):
        at = zc * 64
        w_ref[at : at + 64, :128] = block_ref[zc, :64]
        tail = block_ref[zc, 64:]
        w_ref[at : at + 32, 128:] = tail
        w_ref[at + 32 : at + 64, 128:] = jnp.concatenate([tail[:, 64:], tail[:, :64]], axis=1)


def block_dot(m_ref, w, x):
    at = [pl.ds(pl.multiple_of(z * NX * BLK + x * BLK, BLK), BLK) for z in range(NZ)]
    m = jnp.concatenate([m_ref[:, cols] for cols in at], axis=1)
    return jnp.dot(m, w, preferred_element_type=jnp.float32)


def source(shift):
    return lax.rem(lax.axis_index("x") + (NX - shift), NX)


def some_kernel(shifts, *refs):
    block_refs = refs[: len(shifts)]
    own_ref, other_ref, acc_ref, w_ref = refs[-4:]
    before_ref = refs[len(shifts)] if len(refs) > len(shifts) + 4 else None
    for n, shift in enumerate(shifts):
        spread(block_refs[n], w_ref)
        w = w_ref[...]
        for i, m_ref in enumerate((own_ref, other_ref)):
            part = block_dot(m_ref, w, source(shift))
            if n > 0:
                part += acc_ref[i]
            elif before_ref is not None:
                part += before_ref[i]
            acc_ref[i] = part


def last_kernel(shift, block_ref, in_ref, own_ref, other_ref, out_ref, w_ref, acc_ref):
    spread(block_ref, w_ref)
    w = w_ref[...]
    for i, m_ref in enumerate((own_ref, other_ref)):
        acc_ref[i] = in_ref[i] + block_dot(m_ref, w, source(shift))
    own, other = [(acc_ref[i] * SCALE).T[:HALF] for i in range(NC)]
    leads = lax.axis_index("c") == 0
    sums = jnp.where(leads, own, other), jnp.where(leads, other, own)
    for y in range(NY):
        for c in range(NC):
            at = (y * NC + c) * SEG
            out_ref[at : at + SEG] = sums[c][y * SEG : (y + 1) * SEG]


ACC = (NC, ROWS, 256)
WIDE = NZ * NC * 64


def some_dots(shifts, blocks, before, own, other):
    def some(*refs):
        some_kernel(shifts, *refs)

    return pl.pallas_call(
        some,
        in_specs=[pl.BlockSpec(memory_space=pltpu.VMEM)] * (len(shifts) + len(before) + 2),
        out_specs=pl.BlockSpec(memory_space=pltpu.VMEM),
        out_shape=jax.ShapeDtypeStruct(ACC, jnp.float32),
        scratch_shapes=[pltpu.VMEM((WIDE, 256), jnp.bfloat16)],
        compiler_params=pltpu.CompilerParams(vmem_limit_bytes=16 << 20),
        cost_estimate=pl.CostEstimate(
            flops=len(shifts) * OP * ROWS * COLS // 2, bytes_accessed=3 << 20, transcendentals=0
        ),
    )(*blocks, *before, own, other)


def last_dots(shift, block, acc, own, other):
    def last(*refs):
        last_kernel(shift, *refs)

    return pl.pallas_call(
        last,
        in_specs=[pl.BlockSpec(memory_space=pltpu.VMEM)] * 4,
        out_specs=pl.BlockSpec(memory_space=pltpu.VMEM),
        out_shape=jax.ShapeDtypeStruct((OP, ROWS), jnp.float32),
        scratch_shapes=[pltpu.VMEM((WIDE, 256), jnp.bfloat16), pltpu.VMEM(ACC, jnp.float32)],
        compiler_params=pltpu.CompilerParams(vmem_limit_bytes=16 << 20),
        cost_estimate=pl.CostEstimate(flops=OP * ROWS * COLS // 2, bytes_accessed=3 << 20, transcendentals=0),
    )(block, acc, own, other)


SHIFTS = (2, 1, 3)


def shards(amplitudes, integrals, allowed):
    swap = [(0, 1), (1, 0)]
    raw = lax.ppermute(integrals, "c", swap)
    pieces = pack(amplitudes.T)
    over_z = lax.all_to_all(pieces.reshape(NZ * NC * 96, 128), ("z", "c"), 0, 0, tiled=True)
    block = over_z.reshape(NZ * NC, 96, 128)
    far, right, left = [lax.ppermute(block, "x", [(i, (i + d) % NX) for i in range(NX)]) for d in SHIFTS]
    block, allowed = lax.optimization_barrier((block, allowed))
    own = mask(allowed, integrals)
    other = mask(lax.ppermute(allowed, "c", swap), raw)
    acc = some_dots((0, 2), (block, far), (), own, other)
    acc = some_dots((1,), (right,), (acc,), own, other)
    partial_sums = last_dots(3, left, acc, own, other).astype(jnp.float16)
    landed = lax.all_to_all(partial_sums, ("y", "c"), 0, 0, tiled=True)
    total = jnp.sum(landed.reshape(NY, 2 * SEG, ROWS).astype(jnp.float32), axis=0)
    return (total * (1.0 / SCALE)).astype(jnp.bfloat16)


def solution(mesh):
    fine = Mesh(mesh.devices.reshape(NZ, NX, NC, NY), ("z", "x", "c", "y"))
    vv = ("z", "x", "c")
    placed = (P(None, ("y",) + vv), P(vv, "y"), P(vv, "y"))
    return jax.shard_map(shards, mesh=fine, in_specs=placed, out_specs=P("y", vv), check_vma=False)
```

```python
import jax
import jax.numpy as jnp
from jax import lax
from jax.experimental import pallas as pl
from jax.experimental.pallas import tpu as pltpu
from jax.sharding import Mesh, PartitionSpec as P

OP = 384
BLK = 128
NZ, NX, NC, NY = 8, 4, 2, 8
ROWS = 512
COLS = 4096
HALF = OP // 2
SEG = OP // (NY * NC)
SCALE = 32.0


def pick():
    lane = lax.broadcasted_iota(jnp.int32, (1, 512), 1)
    head = lane < 256
    core = jnp.where(head, lane // 128, (lane - 256) // 128)
    place = jnp.where(head, lane % 128, 128 + lane % 64)
    row = (place // SEG) * (NC * SEG) + core * SEG + place % SEG
    source = lax.broadcasted_iota(jnp.int32, (OP, 512), 0)
    return jnp.where(source == row, 1.0, 0.0).astype(jnp.bfloat16)


def pack_kernel(a_ref, out_ref):
    picked = jnp.dot(a_ref[...], pick(), preferred_element_type=jnp.float32)
    low = lax.broadcasted_iota(jnp.int32, (32, 128), 1) < 64
    for core in range(NC):
        head = picked[:, core * 128 : (core + 1) * 128].astype(jnp.bfloat16)
        both = picked[:, 256 + core * 128 : 256 + (core + 1) * 128]
        tail = jnp.where(low, both[:32], both[32:]).astype(jnp.bfloat16)
        for z in range(NZ):
            out_ref[z, core, :64] = head
            out_ref[z, core, 64:] = tail


def pack(a):
    return pl.pallas_call(
        pack_kernel,
        out_shape=jax.ShapeDtypeStruct((NZ, NC, 96, 128), jnp.bfloat16),
        in_specs=[pl.BlockSpec(memory_space=pltpu.VMEM)],
        out_specs=pl.BlockSpec(memory_space=pltpu.VMEM),
        compiler_params=pltpu.CompilerParams(vmem_limit_bytes=4 << 20),
        cost_estimate=pl.CostEstimate(flops=2 * 64 * OP * 512, bytes_accessed=450_000, transcendentals=0),
    )(a)


def mask_kernel(allowed_ref, m_ref, out_ref):
    @pl.loop(0, ROWS // BLK)
    def _(i):
        rows = pl.ds(pl.multiple_of(i * BLK, BLK), BLK)
        for j in range(COLS // BLK):
            keep = allowed_ref[i, j] != 0
            cols = slice(j * BLK, (j + 1) * BLK)
            tile = m_ref[rows, cols]
            out_ref[rows, cols] = jnp.where(keep, tile, jnp.zeros_like(tile))


def mask(allowed, m):
    return pl.pallas_call(
        mask_kernel,
        in_specs=[pl.BlockSpec(memory_space=pltpu.SMEM), pl.BlockSpec(memory_space=pltpu.VMEM)],
        out_specs=pl.BlockSpec(memory_space=pltpu.VMEM),
        out_shape=jax.ShapeDtypeStruct((ROWS, COLS), jnp.bfloat16),
        compiler_params=pltpu.CompilerParams(vmem_limit_bytes=16 << 20),
        cost_estimate=pl.CostEstimate(flops=ROWS * COLS, bytes_accessed=4 * ROWS * COLS, transcendentals=0),
    )(allowed, m)


def spread(block_ref, w_ref):
    for zc in range(NZ * NC):
        at = zc * 64
        w_ref[at : at + 64, :128] = block_ref[zc, :64]
        tail = block_ref[zc, 64:]
        w_ref[at : at + 32, 128:] = tail
        w_ref[at + 32 : at + 64, 128:] = jnp.concatenate([tail[:, 64:], tail[:, :64]], axis=1)


def block_dot(m_ref, w, x):
    at = [pl.ds(pl.multiple_of(z * NX * BLK + x * BLK, BLK), BLK) for z in range(NZ)]
    m = jnp.concatenate([m_ref[:, cols] for cols in at], axis=1)
    return jnp.dot(m, w, preferred_element_type=jnp.float32)


def source(shift):
    return lax.rem(lax.axis_index("x") + (NX - shift), NX)


def load_kernel(m_ref, after_ref, out_ref, sem):
    del after_ref
    copy = pltpu.make_async_copy(m_ref, out_ref, sem)
    copy.start()
    copy.wait()


def load(m, after):
    return pl.pallas_call(
        load_kernel,
        in_specs=[pl.BlockSpec(memory_space=pl.ANY)] * 2,
        out_specs=pl.BlockSpec(memory_space=pltpu.VMEM),
        out_shape=jax.ShapeDtypeStruct((ROWS, COLS), jnp.bfloat16),
        scratch_shapes=[pltpu.SemaphoreType.DMA],
        compiler_params=pltpu.CompilerParams(vmem_limit_bytes=48 << 20),
        cost_estimate=pl.CostEstimate(flops=0, bytes_accessed=4 * ROWS * COLS, transcendentals=0),
    )(m, after)


def own_kernel(block_ref, own_ref, acc_ref, w_ref):
    spread(block_ref, w_ref)
    acc_ref[...] = block_dot(own_ref, w_ref[...], source(0))


def two_kernel(block_ref, far_ref, acc_own_ref, own_ref, other_ref, acc_ref, w_ref):
    spread(block_ref, w_ref)
    acc_ref[1] = block_dot(other_ref, w_ref[...], source(0))
    spread(far_ref, w_ref)
    w = w_ref[...]
    acc_ref[0] = acc_own_ref[...] + block_dot(own_ref, w, source(2))
    acc_ref[1] += block_dot(other_ref, w, source(2))


def next_kernel(block_ref, in_ref, own_ref, other_ref, acc_ref, w_ref):
    spread(block_ref, w_ref)
    w = w_ref[...]
    for i, m_ref in enumerate((own_ref, other_ref)):
        acc_ref[i] = in_ref[i] + block_dot(m_ref, w, source(1))


def last_kernel(shift, block_ref, in_ref, own_ref, other_ref, out_ref, w_ref, acc_ref):
    spread(block_ref, w_ref)
    w = w_ref[...]
    for i, m_ref in enumerate((own_ref, other_ref)):
        acc_ref[i] = in_ref[i] + block_dot(m_ref, w, source(shift))
    own, other = [(acc_ref[i] * SCALE).T[:HALF] for i in range(NC)]
    leads = lax.axis_index("c") == 0
    sums = jnp.where(leads, own, other), jnp.where(leads, other, own)
    for y in range(NY):
        for c in range(NC):
            at = (y * NC + c) * SEG
            out_ref[at : at + SEG] = sums[c][y * SEG : (y + 1) * SEG]


ACC = (NC, ROWS, 256)
WIDE = NZ * NC * 64


def some_dots(kernel, shape, flops, *args):
    return pl.pallas_call(
        kernel,
        in_specs=[pl.BlockSpec(memory_space=pltpu.VMEM)] * len(args),
        out_specs=pl.BlockSpec(memory_space=pltpu.VMEM),
        out_shape=jax.ShapeDtypeStruct(shape, jnp.float32),
        scratch_shapes=[pltpu.VMEM((WIDE, 256), jnp.bfloat16)],
        compiler_params=pltpu.CompilerParams(vmem_limit_bytes=16 << 20),
        cost_estimate=pl.CostEstimate(flops=flops, bytes_accessed=3 << 20, transcendentals=0),
    )(*args)


def last_dots(shift, block, acc, own, other):
    def last(*refs):
        last_kernel(shift, *refs)

    return pl.pallas_call(
        last,
        in_specs=[pl.BlockSpec(memory_space=pltpu.VMEM)] * 4,
        out_specs=pl.BlockSpec(memory_space=pltpu.VMEM),
        out_shape=jax.ShapeDtypeStruct((OP, ROWS), jnp.float32),
        scratch_shapes=[pltpu.VMEM((WIDE, 256), jnp.bfloat16), pltpu.VMEM(ACC, jnp.float32)],
        compiler_params=pltpu.CompilerParams(vmem_limit_bytes=16 << 20),
        cost_estimate=pl.CostEstimate(flops=OP * ROWS * COLS // 2, bytes_accessed=3 << 20, transcendentals=0),
    )(block, acc, own, other)


SHIFTS = (2, 1, 3)
HIDE = 1 << 36


def shards(amplitudes, integrals, allowed):
    swap = [(0, 1), (1, 0)]
    pieces = pack(amplitudes.T)
    pieces, allowed = lax.optimization_barrier((pieces, allowed))
    over_z = lax.all_to_all(pieces.reshape(NZ * NC * 96, 128), ("z", "c"), 0, 0, tiled=True)
    own = mask(allowed, integrals)
    other = lax.ppermute(own, "c", swap)
    block = over_z.reshape(NZ * NC, 96, 128)
    far, right, left = [lax.ppermute(block, "x", [(i, (i + d) % NX) for i in range(NX)]) for d in SHIFTS]
    acc = some_dots(own_kernel, ACC[1:], HIDE, block, own)
    own, other = load(own, acc), load(other, acc)
    acc = some_dots(two_kernel, ACC, OP * ROWS * COLS, block, far, acc, own, other)
    acc = some_dots(next_kernel, ACC, OP * ROWS * COLS // 2, right, acc, own, other)
    partial_sums = last_dots(3, left, acc, own, other).astype(jnp.float16)
    landed = lax.all_to_all(partial_sums, ("y", "c"), 0, 0, tiled=True)
    total = jnp.sum(landed.reshape(NY, 2 * SEG, ROWS).astype(jnp.float32), axis=0)
    return (total * (1.0 / SCALE)).astype(jnp.bfloat16)


def solution(mesh):
    fine = Mesh(mesh.devices.reshape(NZ, NX, NC, NY), ("z", "x", "c", "y"))
    vv = ("z", "x", "c")
    placed = (P(None, ("y",) + vv), P(vv, "y"), P(vv, "y"))
    return jax.shard_map(shards, mesh=fine, in_specs=placed, out_specs=P("y", vv), check_vma=False)
```

```python
import jax
import jax.numpy as jnp
from jax import lax
from jax.experimental import pallas as pl
from jax.experimental.pallas import tpu as pltpu
from jax.sharding import Mesh, PartitionSpec as P

OP = 384
BLK = 128
NZ, NX, NC, NY = 8, 4, 2, 8
ROWS = 512
COLS = 4096
HALF = OP // 2
SEG = OP // (NY * NC)
SCALE = 32.0


def pick():
    lane = lax.broadcasted_iota(jnp.int32, (1, 512), 1)
    head = lane < 256
    core = jnp.where(head, lane // 128, (lane - 256) // 128)
    place = jnp.where(head, lane % 128, 128 + lane % 64)
    row = (place // SEG) * (NC * SEG) + core * SEG + place % SEG
    source = lax.broadcasted_iota(jnp.int32, (OP, 512), 0)
    return jnp.where(source == row, 1.0, 0.0).astype(jnp.bfloat16)


def pack_kernel(a_ref, out_ref):
    picked = jnp.dot(a_ref[...], pick(), preferred_element_type=jnp.float32)
    low = lax.broadcasted_iota(jnp.int32, (32, 128), 1) < 64
    for core in range(NC):
        head = picked[:, core * 128 : (core + 1) * 128].astype(jnp.bfloat16)
        both = picked[:, 256 + core * 128 : 256 + (core + 1) * 128]
        tail = jnp.where(low, both[:32], both[32:]).astype(jnp.bfloat16)
        for z in range(NZ):
            out_ref[core, z, :64] = head
            out_ref[core, z, 64:] = tail


def pack(a):
    return pl.pallas_call(
        pack_kernel,
        out_shape=jax.ShapeDtypeStruct((NC, NZ, 96, 128), jnp.bfloat16),
        in_specs=[pl.BlockSpec(memory_space=pltpu.VMEM)],
        out_specs=pl.BlockSpec(memory_space=pltpu.VMEM),
        compiler_params=pltpu.CompilerParams(vmem_limit_bytes=4 << 20),
        cost_estimate=pl.CostEstimate(flops=2 * 64 * OP * 512, bytes_accessed=450_000, transcendentals=0),
    )(a)


def mask_kernel(allowed_ref, m_ref, out_ref):
    @pl.loop(0, ROWS // BLK)
    def _(i):
        rows = pl.ds(pl.multiple_of(i * BLK, BLK), BLK)
        for j in range(COLS // BLK):
            keep = allowed_ref[i, j] != 0
            cols = slice(j * BLK, (j + 1) * BLK)
            tile = m_ref[rows, cols]
            out_ref[rows, cols] = jnp.where(keep, tile, jnp.zeros_like(tile))


def mask(allowed, m):
    return pl.pallas_call(
        mask_kernel,
        in_specs=[pl.BlockSpec(memory_space=pltpu.SMEM), pl.BlockSpec(memory_space=pltpu.VMEM)],
        out_specs=pl.BlockSpec(memory_space=pltpu.VMEM),
        out_shape=jax.ShapeDtypeStruct((ROWS, COLS), jnp.bfloat16),
        compiler_params=pltpu.CompilerParams(vmem_limit_bytes=16 << 20),
        cost_estimate=pl.CostEstimate(flops=ROWS * COLS, bytes_accessed=4 * ROWS * COLS, transcendentals=0),
    )(allowed, m)


def spread(block_ref, w_ref):
    for zc in range(NZ * NC):
        at = (zc % NZ * NC + zc // NZ) * 64
        w_ref[at : at + 64, :128] = block_ref[zc, :64]
        tail = block_ref[zc, 64:]
        w_ref[at : at + 32, 128:] = tail
        w_ref[at + 32 : at + 64, 128:] = jnp.concatenate([tail[:, 64:], tail[:, :64]], axis=1)


def block_dot(m_ref, w, x):
    at = [pl.ds(pl.multiple_of(z * NX * BLK + x * BLK, BLK), BLK) for z in range(NZ)]
    m = jnp.concatenate([m_ref[:, cols] for cols in at], axis=1)
    return jnp.dot(m, w, preferred_element_type=jnp.float32)


def source(shift):
    return lax.rem(lax.axis_index("x") + (NX - shift), NX)


def load_kernel(m_ref, after_ref, out_ref, sem):
    del after_ref
    copy = pltpu.make_async_copy(m_ref, out_ref, sem)
    copy.start()
    copy.wait()


def load(m, after):
    return pl.pallas_call(
        load_kernel,
        in_specs=[pl.BlockSpec(memory_space=pl.ANY)] * 2,
        out_specs=pl.BlockSpec(memory_space=pltpu.VMEM),
        out_shape=jax.ShapeDtypeStruct((ROWS, COLS), jnp.bfloat16),
        scratch_shapes=[pltpu.SemaphoreType.DMA],
        compiler_params=pltpu.CompilerParams(vmem_limit_bytes=48 << 20),
        cost_estimate=pl.CostEstimate(flops=0, bytes_accessed=4 * ROWS * COLS, transcendentals=0),
    )(m, after)


def own_kernel(block_ref, own_ref, acc_ref, w_ref):
    spread(block_ref, w_ref)
    acc_ref[...] = block_dot(own_ref, w_ref[...], source(0))


def two_kernel(block_ref, far_ref, acc_own_ref, own_ref, other_ref, acc_ref, w_ref):
    spread(block_ref, w_ref)
    acc_ref[1] = block_dot(other_ref, w_ref[...], source(0))
    spread(far_ref, w_ref)
    w = w_ref[...]
    acc_ref[0] = acc_own_ref[...] + block_dot(own_ref, w, source(2))
    acc_ref[1] += block_dot(other_ref, w, source(2))


def next_kernel(block_ref, in_ref, own_ref, other_ref, acc_ref, w_ref):
    spread(block_ref, w_ref)
    w = w_ref[...]
    for i, m_ref in enumerate((own_ref, other_ref)):
        acc_ref[i] = in_ref[i] + block_dot(m_ref, w, source(1))


def last_kernel(shift, block_ref, in_ref, own_ref, other_ref, out_ref, w_ref, acc_ref):
    spread(block_ref, w_ref)
    w = w_ref[...]
    for i, m_ref in enumerate((own_ref, other_ref)):
        acc_ref[i] = in_ref[i] + block_dot(m_ref, w, source(shift))
    own, other = [(acc_ref[i] * SCALE).T[:HALF] for i in range(NC)]
    leads = lax.axis_index("c") == 0
    sums = jnp.where(leads, own, other), jnp.where(leads, other, own)
    for y in range(NY):
        for c in range(NC):
            at = (c * NY + y) * SEG
            out_ref[at : at + SEG] = sums[c][y * SEG : (y + 1) * SEG]


ACC = (NC, ROWS, 256)
WIDE = NZ * NC * 64


def some_dots(kernel, shape, flops, *args):
    return pl.pallas_call(
        kernel,
        in_specs=[pl.BlockSpec(memory_space=pltpu.VMEM)] * len(args),
        out_specs=pl.BlockSpec(memory_space=pltpu.VMEM),
        out_shape=jax.ShapeDtypeStruct(shape, jnp.float32),
        scratch_shapes=[pltpu.VMEM((WIDE, 256), jnp.bfloat16)],
        compiler_params=pltpu.CompilerParams(vmem_limit_bytes=16 << 20),
        cost_estimate=pl.CostEstimate(flops=flops, bytes_accessed=3 << 20, transcendentals=0),
    )(*args)


def last_dots(shift, block, acc, own, other):
    def last(*refs):
        last_kernel(shift, *refs)

    return pl.pallas_call(
        last,
        in_specs=[pl.BlockSpec(memory_space=pltpu.VMEM)] * 4,
        out_specs=pl.BlockSpec(memory_space=pltpu.VMEM),
        out_shape=jax.ShapeDtypeStruct((OP, ROWS), jnp.float32),
        scratch_shapes=[pltpu.VMEM((WIDE, 256), jnp.bfloat16), pltpu.VMEM(ACC, jnp.float32)],
        compiler_params=pltpu.CompilerParams(vmem_limit_bytes=16 << 20),
        cost_estimate=pl.CostEstimate(flops=OP * ROWS * COLS // 2, bytes_accessed=3 << 20, transcendentals=0),
    )(block, acc, own, other)


SHIFTS = (2, 1, 3)
HIDE = 1 << 36


def shards(amplitudes, integrals, allowed):
    swap = [(0, 1), (1, 0)]
    pieces = pack(amplitudes.T)
    pieces, allowed = lax.optimization_barrier((pieces, allowed))
    over_z = lax.all_to_all(pieces.reshape(NZ * NC * 96, 128), ("c", "z"), 0, 0, tiled=True)
    own = mask(allowed, integrals)
    other = lax.ppermute(own, "c", swap)
    block = over_z.reshape(NZ * NC, 96, 128)
    far, right, left = [lax.ppermute(block, "x", [(i, (i + d) % NX) for i in range(NX)]) for d in SHIFTS]
    acc = some_dots(own_kernel, ACC[1:], HIDE, block, own)
    own, other = load(own, acc), load(other, acc)
    acc = some_dots(two_kernel, ACC, OP * ROWS * COLS, block, far, acc, own, other)
    acc = some_dots(next_kernel, ACC, OP * ROWS * COLS // 2, right, acc, own, other)
    partial_sums = last_dots(3, left, acc, own, other).astype(jnp.float16)
    landed = lax.all_to_all(partial_sums, ("c", "y"), 0, 0, tiled=True)
    total = jnp.sum(landed.reshape(NC, NY, SEG, ROWS).astype(jnp.float32), axis=1).reshape(NC * SEG, ROWS)
    return (total * (1.0 / SCALE)).astype(jnp.bfloat16)


def solution(mesh):
    fine = Mesh(mesh.devices.reshape(NZ, NX, NC, NY), ("z", "x", "c", "y"))
    vv = ("z", "x", "c")
    placed = (P(None, ("y",) + vv), P(vv, "y"), P(vv, "y"))
    return jax.shard_map(shards, mesh=fine, in_specs=placed, out_specs=P("y", vv), check_vma=False)
```

```python
import jax
import jax.numpy as jnp
from jax import lax
from jax.experimental import pallas as pl
from jax.experimental.pallas import tpu as pltpu
from jax.sharding import Mesh, PartitionSpec as P

OP = 384
BLK = 128
NZ, NX, NC, NY = 8, 4, 2, 8
ROWS = 512
COLS = 4096
HALF = OP // 2
SEG = OP // (NY * NC)
SCALE = 32.0


def pick():
    lane = lax.broadcasted_iota(jnp.int32, (1, 512), 1)
    head = lane < 256
    core = jnp.where(head, lane // 128, (lane - 256) // 128)
    place = jnp.where(head, lane % 128, 128 + lane % 64)
    row = (place // SEG) * (NC * SEG) + core * SEG + place % SEG
    source = lax.broadcasted_iota(jnp.int32, (OP, 512), 0)
    return jnp.where(source == row, 1.0, 0.0).astype(jnp.bfloat16)


def pack_kernel(a_ref, out_ref):
    picked = jnp.dot(a_ref[...], pick(), preferred_element_type=jnp.float32)
    low = lax.broadcasted_iota(jnp.int32, (32, 128), 1) < 64
    for core in range(NC):
        head = picked[:, core * 128 : (core + 1) * 128].astype(jnp.bfloat16)
        both = picked[:, 256 + core * 128 : 256 + (core + 1) * 128]
        tail = jnp.where(low, both[:32], both[32:]).astype(jnp.bfloat16)
        for z in range(NZ):
            out_ref[core, z, :64] = head
            out_ref[core, z, 64:] = tail


def pack(a):
    return pl.pallas_call(
        pack_kernel,
        out_shape=jax.ShapeDtypeStruct((NC, NZ, 96, 128), jnp.bfloat16),
        in_specs=[pl.BlockSpec(memory_space=pltpu.VMEM)],
        out_specs=pl.BlockSpec(memory_space=pltpu.VMEM),
        compiler_params=pltpu.CompilerParams(vmem_limit_bytes=4 << 20),
        cost_estimate=pl.CostEstimate(flops=2 * 64 * OP * 512, bytes_accessed=450_000, transcendentals=0),
    )(a)


def mask_kernel(allowed_ref, m_ref, out_ref):
    @pl.loop(0, ROWS // BLK)
    def _(i):
        rows = pl.ds(pl.multiple_of(i * BLK, BLK), BLK)
        for j in range(COLS // BLK):
            keep = allowed_ref[i, j] != 0
            cols = slice(j * BLK, (j + 1) * BLK)
            tile = m_ref[rows, cols]
            out_ref[rows, cols] = jnp.where(keep, tile, jnp.zeros_like(tile))


def mask(allowed, m):
    return pl.pallas_call(
        mask_kernel,
        in_specs=[pl.BlockSpec(memory_space=pltpu.SMEM), pl.BlockSpec(memory_space=pltpu.VMEM)],
        out_specs=pl.BlockSpec(memory_space=pltpu.VMEM),
        out_shape=jax.ShapeDtypeStruct((ROWS, COLS), jnp.bfloat16),
        compiler_params=pltpu.CompilerParams(vmem_limit_bytes=16 << 20),
        cost_estimate=pl.CostEstimate(flops=ROWS * COLS, bytes_accessed=4 * ROWS * COLS, transcendentals=0),
    )(allowed, m)


def spread(block_ref, w_ref):
    for zc in range(NZ * NC):
        at = (zc % NZ * NC + zc // NZ) * 64
        w_ref[at : at + 64, :128] = block_ref[zc, :64]
        tail = block_ref[zc, 64:]
        w_ref[at : at + 32, 128:] = tail
        w_ref[at + 32 : at + 64, 128:] = jnp.concatenate([tail[:, 64:], tail[:, :64]], axis=1)


def block_dot(m_ref, w, x):
    at = [pl.ds(pl.multiple_of(z * NX * BLK + x * BLK, BLK), BLK) for z in range(NZ)]
    m = jnp.concatenate([m_ref[:, cols] for cols in at], axis=1)
    return jnp.dot(m, w, preferred_element_type=jnp.float32)


def source(shift):
    return lax.rem(lax.axis_index("x") + (NX - shift), NX)


def load_kernel(m_ref, after_ref, out_ref, sem):
    del after_ref
    copy = pltpu.make_async_copy(m_ref, out_ref, sem)
    copy.start()
    copy.wait()


def load(m, after):
    return pl.pallas_call(
        load_kernel,
        in_specs=[pl.BlockSpec(memory_space=pl.ANY)] * 2,
        out_specs=pl.BlockSpec(memory_space=pltpu.VMEM),
        out_shape=jax.ShapeDtypeStruct((ROWS, COLS), jnp.bfloat16),
        scratch_shapes=[pltpu.SemaphoreType.DMA],
        compiler_params=pltpu.CompilerParams(vmem_limit_bytes=48 << 20),
        cost_estimate=pl.CostEstimate(flops=0, bytes_accessed=4 * ROWS * COLS, transcendentals=0),
    )(m, after)


def own_kernel(block_ref, own_ref, acc_ref, w_ref):
    spread(block_ref, w_ref)
    acc_ref[...] = block_dot(own_ref, w_ref[...], source(0))


def two_kernel(block_ref, far_ref, acc_own_ref, own_ref, other_ref, acc_ref, w_ref):
    spread(block_ref, w_ref)
    acc_ref[1] = block_dot(other_ref, w_ref[...], source(0))
    spread(far_ref, w_ref)
    w = w_ref[...]
    acc_ref[0] = acc_own_ref[...] + block_dot(own_ref, w, source(2))
    acc_ref[1] += block_dot(other_ref, w, source(2))


def last_kernel(shifts, first_ref, second_ref, in_ref, own_ref, other_ref, out_ref, w_ref, acc_ref):
    for n, block_ref in enumerate((first_ref, second_ref)):
        spread(block_ref, w_ref)
        w = w_ref[...]
        for i, m_ref in enumerate((own_ref, other_ref)):
            before = in_ref[i] if n == 0 else acc_ref[i]
            acc_ref[i] = before + block_dot(m_ref, w, source(shifts[n]))
    own, other = [(acc_ref[i] * SCALE).T[:HALF] for i in range(NC)]
    leads = lax.axis_index("c") == 0
    sums = jnp.where(leads, own, other), jnp.where(leads, other, own)
    for y in range(NY):
        for c in range(NC):
            at = (c * NY + y) * SEG
            out_ref[at : at + SEG] = sums[c][y * SEG : (y + 1) * SEG]


ACC = (NC, ROWS, 256)
WIDE = NZ * NC * 64


def some_dots(kernel, shape, flops, *args):
    return pl.pallas_call(
        kernel,
        in_specs=[pl.BlockSpec(memory_space=pltpu.VMEM)] * len(args),
        out_specs=pl.BlockSpec(memory_space=pltpu.VMEM),
        out_shape=jax.ShapeDtypeStruct(shape, jnp.float32),
        scratch_shapes=[pltpu.VMEM((WIDE, 256), jnp.bfloat16)],
        compiler_params=pltpu.CompilerParams(vmem_limit_bytes=16 << 20),
        cost_estimate=pl.CostEstimate(flops=flops, bytes_accessed=3 << 20, transcendentals=0),
    )(*args)


def last_dots(shifts, blocks, acc, own, other):
    def last(*refs):
        last_kernel(shifts, *refs)

    return pl.pallas_call(
        last,
        in_specs=[pl.BlockSpec(memory_space=pltpu.VMEM)] * 5,
        out_specs=pl.BlockSpec(memory_space=pltpu.VMEM),
        out_shape=jax.ShapeDtypeStruct((OP, ROWS), jnp.float32),
        scratch_shapes=[pltpu.VMEM((WIDE, 256), jnp.bfloat16), pltpu.VMEM(ACC, jnp.float32)],
        compiler_params=pltpu.CompilerParams(vmem_limit_bytes=16 << 20),
        cost_estimate=pl.CostEstimate(flops=OP * ROWS * COLS, bytes_accessed=3 << 20, transcendentals=0),
    )(*blocks, acc, own, other)


SHIFTS = (2, 1, 3)
HIDE = 1 << 36


def shards(amplitudes, integrals, allowed):
    swap = [(0, 1), (1, 0)]
    pieces = pack(amplitudes.T)
    pieces, allowed = lax.optimization_barrier((pieces, allowed))
    over_z = lax.all_to_all(pieces.reshape(NZ * NC * 96, 128), ("c", "z"), 0, 0, tiled=True)
    own = mask(allowed, integrals)
    other = lax.ppermute(own, "c", swap)
    block = over_z.reshape(NZ * NC, 96, 128)
    far, right, left = [lax.ppermute(block, "x", [(i, (i + d) % NX) for i in range(NX)]) for d in SHIFTS]
    acc = some_dots(own_kernel, ACC[1:], HIDE, block, own)
    own, other = load(own, acc), load(other, acc)
    acc = some_dots(two_kernel, ACC, OP * ROWS * COLS, block, far, acc, own, other)
    partial_sums = last_dots((1, 3), (right, left), acc, own, other).astype(jnp.float16)
    landed = lax.all_to_all(partial_sums, ("c", "y"), 0, 0, tiled=True)
    total = jnp.sum(landed.reshape(NC, NY, SEG, ROWS).astype(jnp.float32), axis=1).reshape(NC * SEG, ROWS)
    return (total * (1.0 / SCALE)).astype(jnp.bfloat16)


def solution(mesh):
    fine = Mesh(mesh.devices.reshape(NZ, NX, NC, NY), ("z", "x", "c", "y"))
    vv = ("z", "x", "c")
    placed = (P(None, ("y",) + vv), P(vv, "y"), P(vv, "y"))
    return jax.shard_map(shards, mesh=fine, in_specs=placed, out_specs=P("y", vv), check_vma=False)
```

```python
import jax
import jax.numpy as jnp
from jax import lax
from jax.experimental import pallas as pl
from jax.experimental.pallas import tpu as pltpu
from jax.sharding import Mesh, PartitionSpec as P

OP = 384
BLK = 128
NZ, NX, NC, NY = 8, 4, 2, 8
ROWS = 512
COLS = 4096
HALF = OP // 2
SEG = OP // (NY * NC)
SCALE = 32.0


def pick():
    lane = lax.broadcasted_iota(jnp.int32, (1, 512), 1)
    head = lane < 256
    core = jnp.where(head, lane // 128, (lane - 256) // 128)
    place = jnp.where(head, lane % 128, 128 + lane % 64)
    row = (place // SEG) * (NC * SEG) + core * SEG + place % SEG
    source = lax.broadcasted_iota(jnp.int32, (OP, 512), 0)
    return jnp.where(source == row, 1.0, 0.0).astype(jnp.bfloat16)


def pack_kernel(a_ref, out_ref):
    picked = jnp.dot(a_ref[...], pick(), preferred_element_type=jnp.float32)
    low = lax.broadcasted_iota(jnp.int32, (32, 128), 1) < 64
    for core in range(NC):
        head = picked[:, core * 128 : (core + 1) * 128].astype(jnp.bfloat16)
        both = picked[:, 256 + core * 128 : 256 + (core + 1) * 128]
        tail = jnp.where(low, both[:32], both[32:]).astype(jnp.bfloat16)
        for z in range(NZ):
            out_ref[core, z, :64] = head
            out_ref[core, z, 64:] = tail


def pack(a):
    return pl.pallas_call(
        pack_kernel,
        out_shape=jax.ShapeDtypeStruct((NC, NZ, 96, 128), jnp.bfloat16),
        in_specs=[pl.BlockSpec(memory_space=pltpu.VMEM)],
        out_specs=pl.BlockSpec(memory_space=pltpu.VMEM),
        compiler_params=pltpu.CompilerParams(vmem_limit_bytes=4 << 20),
        cost_estimate=pl.CostEstimate(flops=2 * 64 * OP * 512, bytes_accessed=450_000, transcendentals=0),
    )(a)


def mask_kernel(allowed_ref, m_ref, out_ref):
    @pl.loop(0, ROWS // BLK)
    def _(i):
        rows = pl.ds(pl.multiple_of(i * BLK, BLK), BLK)
        for j in range(COLS // BLK):
            keep = allowed_ref[i, j] != 0
            cols = slice(j * BLK, (j + 1) * BLK)
            tile = m_ref[rows, cols]
            out_ref[rows, cols] = jnp.where(keep, tile, jnp.zeros_like(tile))


def mask(allowed, m):
    return pl.pallas_call(
        mask_kernel,
        in_specs=[pl.BlockSpec(memory_space=pltpu.SMEM), pl.BlockSpec(memory_space=pltpu.VMEM)],
        out_specs=pl.BlockSpec(memory_space=pltpu.VMEM),
        out_shape=jax.ShapeDtypeStruct((ROWS, COLS), jnp.bfloat16),
        compiler_params=pltpu.CompilerParams(vmem_limit_bytes=16 << 20),
        cost_estimate=pl.CostEstimate(flops=ROWS * COLS, bytes_accessed=4 * ROWS * COLS, transcendentals=0),
    )(allowed, m)


def spread(block_ref, w_ref):
    for zc in range(NZ * NC):
        at = (zc % NZ * NC + zc // NZ) * 64
        w_ref[at : at + 64, :128] = block_ref[zc, :64]
        tail = block_ref[zc, 64:]
        w_ref[at : at + 32, 128:] = tail
        w_ref[at + 32 : at + 64, 128:] = jnp.concatenate([tail[:, 64:], tail[:, :64]], axis=1)


def block_dot(m_ref, w, x):
    at = [pl.ds(pl.multiple_of(z * NX * BLK + x * BLK, BLK), BLK) for z in range(NZ)]
    m = jnp.concatenate([m_ref[:, cols] for cols in at], axis=1)
    return jnp.dot(m, w, preferred_element_type=jnp.float32)


def source(shift):
    return lax.rem(lax.axis_index("x") + (NX - shift), NX)


def load_kernel(m_ref, after_ref, out_ref, sem):
    del after_ref
    copy = pltpu.make_async_copy(m_ref, out_ref, sem)
    copy.start()
    copy.wait()


def load(m, after):
    return pl.pallas_call(
        load_kernel,
        in_specs=[pl.BlockSpec(memory_space=pl.ANY)] * 2,
        out_specs=pl.BlockSpec(memory_space=pltpu.VMEM),
        out_shape=jax.ShapeDtypeStruct((ROWS, COLS), jnp.bfloat16),
        scratch_shapes=[pltpu.SemaphoreType.DMA],
        compiler_params=pltpu.CompilerParams(vmem_limit_bytes=48 << 20),
        cost_estimate=pl.CostEstimate(flops=0, bytes_accessed=4 * ROWS * COLS, transcendentals=0),
    )(m, after)


def own_kernel(block_ref, own_ref, acc_ref, w_ref):
    spread(block_ref, w_ref)
    acc_ref[...] = block_dot(own_ref, w_ref[...], source(0))


def two_kernel(block_ref, far_ref, acc_own_ref, own_ref, other_ref, acc_ref, w_ref):
    spread(block_ref, w_ref)
    acc_ref[1] = block_dot(other_ref, w_ref[...], source(0))
    spread(far_ref, w_ref)
    w = w_ref[...]
    acc_ref[0] = acc_own_ref[...] + block_dot(own_ref, w, source(2))
    acc_ref[1] += block_dot(other_ref, w, source(2))


def next_kernel(block_ref, in_ref, own_ref, other_ref, acc_ref, w_ref):
    spread(block_ref, w_ref)
    w = w_ref[...]
    for i, m_ref in enumerate((own_ref, other_ref)):
        acc_ref[i] = in_ref[i] + block_dot(m_ref, w, source(1))


def last_kernel(shift, block_ref, in_ref, own_ref, other_ref, out_ref, w_ref, acc_ref):
    spread(block_ref, w_ref)
    w = w_ref[...]
    for i, m_ref in enumerate((own_ref, other_ref)):
        acc_ref[i] = in_ref[i] + block_dot(m_ref, w, source(shift))
    own, other = [(acc_ref[i] * SCALE).T[:HALF] for i in range(NC)]
    leads = lax.axis_index("c") == 0
    sums = jnp.where(leads, own, other), jnp.where(leads, other, own)
    for y in range(NY):
        for c in range(NC):
            at = (c * NY + y) * SEG
            out_ref[at : at + SEG] = sums[c][y * SEG : (y + 1) * SEG]


ACC = (NC, ROWS, 256)
WIDE = NZ * NC * 64


def some_dots(kernel, shape, flops, *args):
    return pl.pallas_call(
        kernel,
        in_specs=[pl.BlockSpec(memory_space=pltpu.VMEM)] * len(args),
        out_specs=pl.BlockSpec(memory_space=pltpu.VMEM),
        out_shape=jax.ShapeDtypeStruct(shape, jnp.float32),
        scratch_shapes=[pltpu.VMEM((WIDE, 256), jnp.bfloat16)],
        compiler_params=pltpu.CompilerParams(vmem_limit_bytes=16 << 20),
        cost_estimate=pl.CostEstimate(flops=flops, bytes_accessed=3 << 20, transcendentals=0),
    )(*args)


def last_dots(shift, block, acc, own, other):
    def last(*refs):
        last_kernel(shift, *refs)

    return pl.pallas_call(
        last,
        in_specs=[pl.BlockSpec(memory_space=pltpu.VMEM)] * 4,
        out_specs=pl.BlockSpec(memory_space=pltpu.VMEM),
        out_shape=jax.ShapeDtypeStruct((OP, ROWS), jnp.float32),
        scratch_shapes=[pltpu.VMEM((WIDE, 256), jnp.bfloat16), pltpu.VMEM(ACC, jnp.float32)],
        compiler_params=pltpu.CompilerParams(vmem_limit_bytes=16 << 20),
        cost_estimate=pl.CostEstimate(flops=OP * ROWS * COLS // 2, bytes_accessed=3 << 20, transcendentals=0),
    )(block, acc, own, other)


SHIFTS = (2, 1, 3)
HIDE = 1 << 36


def shards(amplitudes, integrals, allowed):
    swap = [(0, 1), (1, 0)]
    pieces = pack(amplitudes.T)
    pieces, allowed = lax.optimization_barrier((pieces, allowed))
    over_z = lax.all_to_all(pieces.reshape(NZ * NC * 96, 128), ("c", "z"), 0, 0, tiled=True)
    own = mask(allowed, integrals)
    other = lax.ppermute(own, "c", swap)
    block = over_z.reshape(NZ * NC, 96, 128)
    far, right, left = [lax.ppermute(block, "x", [(i, (i + d) % NX) for i in range(NX)]) for d in SHIFTS]
    acc = some_dots(own_kernel, ACC[1:], HIDE, block, own)
    own, other = load(own, acc), load(other, acc)
    acc = some_dots(two_kernel, ACC, OP * ROWS * COLS, block, far, acc, own, other)
    acc = some_dots(next_kernel, ACC, OP * ROWS * COLS // 2, right, acc, own, other)
    partial_sums = last_dots(3, left, acc, own, other).astype(jnp.float16)
    landed = lax.all_to_all(partial_sums, ("c", "y"), 0, 0, tiled=True)
    parts = landed.reshape(NC, NY, SEG, ROWS).astype(jnp.float32) * (1.0 / SCALE)
    return jnp.sum(parts, axis=1).reshape(NC * SEG, ROWS).astype(jnp.bfloat16)


def solution(mesh):
    fine = Mesh(mesh.devices.reshape(NZ, NX, NC, NY), ("z", "x", "c", "y"))
    vv = ("z", "x", "c")
    placed = (P(None, ("y",) + vv), P(vv, "y"), P(vv, "y"))
    return jax.shard_map(shards, mesh=fine, in_specs=placed, out_specs=P("y", vv), check_vma=False)
```
